32 devices in a mesh: ctx: 8 (over z, x), head: 4 (over y, core).
Axes of the slice: x: 2, y: 2, z: 4, core: 2. Of those that a mesh axis runs over, the one named last changes fastest.
Arguments:
- queries: bfloat16 [8192, 1024], P(('ctx', 'head')), may hold values from -6 to 6
- keys: bfloat16 [8192, 1024], P(('ctx', 'head')), may hold values from -6 to 6
- values: bfloat16 [8192, 1024], P(('ctx', 'head')), may hold values from -6 to 6
- grads_out: bfloat16 [8192, 1024], P(('ctx', 'head')), may hold values from -6 to 6
- log_decay: float32 [8, 8192], P('head', 'ctx'), may hold values from -0.8 to 0
- ridge: float32 [8], P('head'), may hold values from 0.25 to 2
Outputs:
- grad_queries: bfloat16 [8192, 1024], P(('ctx', 'head'))
- grad_keys: bfloat16 [8192, 1024], P(('ctx', 'head'))
- grad_values: bfloat16 [8192, 1024], P(('ctx', 'head'))
The draws below stay inside these ranges and needn't reach their ends.
All inputs are finite; a program needn't handle non-finite values.
Results may differ from the reference program's by a relative error of at most 0.0085.
Values may be sent and summed in bfloat16 or wider, within the bound.
A program may use at most 128 MiB of HBM per device.

```python
import math
import jax
import jax.numpy as jnp
from jax import lax

DH = 128
SPAN = 512
SOLVE_STEPS = 8
HEADS = 8
TOKEN_COUNT = 8192


def draw_keys(key, part):
    scale_key = jax.random.fold_in(key, 11)
    base_key = jax.random.fold_in(key, 12)
    columns = jnp.exp(jax.random.uniform(scale_key, (HEADS * DH,), jnp.float32, jnp.log(0.05), jnp.log(1.5)))
    overall = 5.0 / jnp.sqrt(jnp.float32(TOKEN_COUNT))
    base = jnp.clip(jax.random.normal(base_key, (TOKEN_COUNT, HEADS * DH), jnp.float32), -4.0, 4.0)
    return (base * columns[None, :] * overall).astype(jnp.bfloat16)


def draw_log_decay(key, part):
    share = 0.5
    fast = jax.random.uniform(jax.random.fold_in(key, 21), (HEADS, 1), jnp.float32) < share
    base = jnp.where(fast, 1.0 / 40.0, 0.5 / TOKEN_COUNT)
    jitter = jax.random.uniform(jax.random.fold_in(key, 22), (HEADS, TOKEN_COUNT), jnp.float32, 0.5, 1.5)
    region = jnp.exp(jax.random.uniform(jax.random.fold_in(key, 23), (HEADS, 8), jnp.float32, jnp.log(0.5), jnp.log(2.0)))
    spread = jnp.repeat(region, TOKEN_COUNT // 8, axis=1)
    segment_batches = jax.random.randint(jax.random.fold_in(key, 24), (3,), 0, TOKEN_COUNT)
    token_offsets = jnp.arange(TOKEN_COUNT, dtype=jnp.int32)
    masked_out_cells = jnp.any(token_offsets[None, :] == segment_batches[:, None], axis=0)
    drops = jax.random.uniform(jax.random.fold_in(key, 25), (HEADS, TOKEN_COUNT), jnp.float32, 0.22, 0.69)
    rate = base * jitter * spread + jnp.where(masked_out_cells[None, :], drops, 0.0)
    return (-rate).astype(jnp.float32)


def level_of(stream_key, extent, shards, low, largest):
    def one(dim, parts):
        heights = jax.random.uniform(jax.random.fold_in(jax.random.fold_in(stream_key, 6), dim), (parts,), jnp.float32, low / len(shards), largest / len(shards))
        return jnp.repeat(jnp.exp(heights), extent[dim] // parts).reshape((-1,) + (1,) * (len(extent) - dim - 1))

    level = one(*shards[0])
    for cut in shards[1:]:
        level = level * one(*cut)
    return level


def noise(stream_key, extent, scale, limit, pieces=(), kind=jnp.bfloat16):
    array = jax.random.normal(stream_key, extent, jnp.float32) * scale
    if len(pieces) > 0:
        array = level_of(stream_key, extent, pieces, -0.22, 0.18) * array
    return jnp.clip(array, min=-limit, max=limit).astype(kind)


def setup_inputs(seed: int = 0) -> dict:
    key_of = jax.random.split(jax.random.key(seed), 7)
    return {
        "queries": noise(key_of[0], (TOKEN_COUNT, HEADS * DH), 1.0, 6.0, ((0, 32),)),
        "keys": draw_keys(jax.random.fold_in(key_of[6], 71), 0),
        "values": noise(key_of[2], (TOKEN_COUNT, HEADS * DH), 1.0, 6.0, ((0, 32),)),
        "grads_out": noise(key_of[3], (TOKEN_COUNT, HEADS * DH), 1.0, 6.0, ((0, 32),)),
        "log_decay": draw_log_decay(jax.random.fold_in(key_of[6], 71), 0),
        "ridge": jnp.clip(jnp.exp(math.log(2.0) - 2.0794415 * jax.random.uniform(key_of[5], (HEADS,), jnp.float32) ** level_of(key_of[5], (HEADS,), ((0, 4),), -0.2, 0.2)), 0.25, 2.0),
    }


highest = lax.Precision.HIGHEST
epsilon = 1e-06

def product(left, right):
    return jnp.dot(left.astype(jnp.float32), right.astype(jnp.float32), precision=highest, preferred_element_type=jnp.float32)

def mixed(left, right):
    return jnp.dot(left.astype(jnp.bfloat16), right.astype(jnp.bfloat16), preferred_element_type=jnp.float32)

def block_decays(log_gate):
    cumul = jnp.cumsum(log_gate)
    size = log_gate.shape[0]
    rowpos = lax.broadcasted_iota(jnp.int32, (size, size), 0)
    column_position = lax.broadcasted_iota(jnp.int32, (size, size), 1)
    within = jnp.exp(jnp.where(rowpos >= column_position, cumul[:, None] - cumul[None, :], -jnp.inf))
    return (cumul, within)

def multiply_by_matrix(direction, gram, keys, within, start_decay, ridge):
    scores = (within * mixed(direction.astype(jnp.bfloat16), keys.T)).astype(jnp.bfloat16)
    return start_decay[:, None] * product(direction, gram) + mixed(scores, keys) + ridge * direction

def conj_grad(rhs, gram, keys, within, start_decay, ridge):
    solution = jnp.zeros_like(rhs)
    residual = rhs
    direction = rhs
    rho_now = lax.optimization_barrier(jnp.sum(rhs * rhs, axis=-1, keepdims=True))
    for sweep in range(SOLVE_STEPS):
        image = multiply_by_matrix(direction, gram, keys, within, start_decay, ridge)
        step_size = rho_now / (lax.optimization_barrier(jnp.sum(direction * image, axis=-1, keepdims=True)) + epsilon)
        solution = solution + step_size * direction
        residual = residual - step_size * image
        rho_next = lax.optimization_barrier(jnp.sum(residual * residual, axis=-1, keepdims=True))
        direction = residual + rho_next / (rho_now + epsilon) * direction
        rho_now = rho_next
    return solution

def span_solve(gram, value_state, queries, keys, values, grads_out, log_gate, ridge):
    cumul, within = block_decays(log_gate)
    start_decay = jnp.exp(cumul)
    solved = conj_grad(queries.astype(jnp.float32), gram, keys, within, start_decay, ridge)
    scores = (within * mixed(grads_out, values.T)).astype(jnp.bfloat16)
    rhs = start_decay[:, None] * product(grads_out, value_state) + mixed(scores, keys)
    adjoint = conj_grad(rhs, gram, keys, within, start_decay, ridge)
    return (solved, adjoint)

def span_grads(value_memory_state, state_gram, keys, values, grads_out, solved, adjoint, log_gate):
    cumul, within = block_decays(log_gate)
    end_weight = jnp.exp(cumul[-1] - cumul)[:, None]
    solved_low = solved.astype(jnp.bfloat16)
    adjoint_low = adjoint.astype(jnp.bfloat16)
    solved_along_keys = (within * mixed(solved_low, keys.T)).astype(jnp.bfloat16)
    along_adjoint = (within * mixed(adjoint_low, keys.T)).astype(jnp.bfloat16)
    along_values = (within * mixed(grads_out, values.T)).astype(jnp.bfloat16)
    grad_values = mixed(solved_along_keys.T, grads_out) + end_weight * product(keys, value_memory_state.T)
    grad_keys = mixed(along_values.T, solved_low) + end_weight * product(values, value_memory_state)
    grad_keys = grad_keys - mixed(solved_along_keys.T, adjoint_low) - mixed(along_adjoint.T, solved_low)
    grad_keys = grad_keys + end_weight * product(keys, state_gram + state_gram.T)
    return (grad_keys, grad_values)

def one_head(pack):
    queries, keys, values, grads_out, log_gate, ridge = pack
    zeros = jnp.zeros((DH, DH), jnp.float32)

    def forward(carry, items):
        gram, value_state = carry
        qblock, kblock, vblock, gblock, lower_tile = items
        solved, adjoint = span_solve(gram, value_state, qblock, kblock, vblock, gblock, lower_tile, ridge)
        cumul = jnp.cumsum(lower_tile)
        weighted = jnp.exp(cumul[-1] - cumul)[:, None] * kblock.astype(jnp.float32)
        total = jnp.exp(cumul[-1])
        gram_next = total * gram + product(kblock.T, weighted)
        value_next = total * value_state + product(vblock.T, weighted)
        return ((gram_next, value_next), (solved, adjoint))
    init = (zeros, zeros)
    unused, outs = lax.scan(forward, init, (queries, keys, values, grads_out, log_gate))
    solved, adjoint = outs

    def backward(carry, items):
        value_memory_state, state_gram = carry
        kblock, vblock, gblock, sblock, ablock, lower_tile = items
        grad_keys, grad_values = span_grads(value_memory_state, state_gram, kblock, vblock, gblock, sblock, ablock, lower_tile)
        cumul = jnp.cumsum(lower_tile)
        weighted = jnp.exp(cumul)[:, None] * sblock
        total = jnp.exp(cumul[-1])
        value_prev = total * value_memory_state + product(gblock.T, weighted)
        gram_prev = total * state_gram - product(ablock.T, weighted)
        return ((value_prev, gram_prev), (grad_keys, grad_values))
    unused2, grads = lax.scan(backward, init, (keys, values, grads_out, solved, adjoint, log_gate), reverse=True)
    return (adjoint, grads[0], grads[1])

def split_all(block):
    count = TOKEN_COUNT // SPAN
    return block.reshape(count, SPAN, HEADS, DH).transpose(2, 0, 1, 3)

def join_all(block):
    return block.transpose(1, 2, 0, 3).reshape(TOKEN_COUNT, HEADS * DH).astype(jnp.bfloat16)

def reference(queries, keys, values, grads_out, log_decay, ridge):
    count = TOKEN_COUNT // SPAN
    gates = log_decay.reshape(HEADS, count, SPAN)
    pack = (split_all(queries), split_all(keys), split_all(values), split_all(grads_out), gates, ridge)
    adjoint, grad_keys, grad_values = lax.map(one_head, pack)
    return (join_all(adjoint), join_all(grad_keys), join_all(grad_values))
```

```python
import functools

import jax
import jax.numpy as jnp
from jax import lax
from jax.experimental import pallas as pl
from jax.experimental.pallas import tpu as pltpu
from jax.sharding import PartitionSpec as P

DH = 128
SPAN = 512
SOLVE_STEPS = 8


highest = lax.Precision.HIGHEST
epsilon = 1e-06


CHUNK = 256
WORK_BYTES = 48 * 1024 * 1024


def dot(left, right, dims):
    return lax.dot_general(left, right, (dims, ((), ())), preferred_element_type=jnp.float32)


def dot_nn(left, right):
    return dot(left, right, ((1,), (0,)))


def dot_nt(left, right):
    return dot(left, right, ((1,), (1,)))


def dot_tn(left, right):
    return dot(left, right, ((0,), (0,)))


def low(array):
    return array.astype(jnp.bfloat16)


def two_parts(array):
    high = low(array)
    return high, low(array - high.astype(jnp.float32))


def running_sums(gate_row):
    size = gate_row.shape[1]
    rowpos = lax.broadcasted_iota(jnp.int32, (size, size), 0)
    column_position = lax.broadcasted_iota(jnp.int32, (size, size), 1)
    spread = jnp.broadcast_to(gate_row, (size, size))
    column = jnp.sum(jnp.where(rowpos >= column_position, spread, 0.0), axis=1, keepdims=True)
    gate_column = jnp.sum(jnp.where(rowpos == column_position, spread, 0.0), axis=1, keepdims=True)
    row = jnp.sum(jnp.where(rowpos <= column_position, gate_column, 0.0), axis=0, keepdims=True)
    return column, row, rowpos >= column_position


def solve_kernel(
    count, ridge_ref, gate_ref, q_ref, k_ref, v_ref, g_ref, gram_ref, value_ref,
    low_x_ref, low_y_ref, part_keys_ref, part_values_ref, value_back_ref, gram_back_ref,
    within_ref, decay_ref, stack_ref, x_ref, r_ref, p_ref, rho_ref,
):
    ridge = ridge_ref[pl.program_id(0) // count]
    column, row, causal = running_sums(gate_ref[0])
    within_ref[...] = jnp.where(causal, jnp.exp(jnp.minimum(column - row, 0.0)), 0.0)
    decay_ref[...] = jnp.broadcast_to(jnp.exp(column), decay_ref.shape)
    gram_high, gram_low = two_parts(gram_ref[0])
    stack_ref[0:DH] = gram_high
    stack_ref[DH : 2 * DH] = gram_high
    stack_ref[2 * DH : 3 * DH] = gram_low
    value_high, value_low = two_parts(value_ref[0])
    span = q_ref.shape[0]
    chunks = [(start, start + CHUNK) for start in range(0, span, CHUNK)]
    for start, stop in chunks:
        rows = slice(start, stop)
        grads = g_ref[rows]
        scores = low(within_ref[rows, 0:stop] * dot_nt(grads, v_ref[0:stop]))
        state = dot_nn(grads, value_high) + dot_nn(grads, value_low)
        rhs = decay_ref[rows] * state + dot_nn(scores, k_ref[0:stop])
        for side, first in enumerate((q_ref[rows].astype(jnp.float32), rhs)):
            x_ref[side, rows] = jnp.zeros_like(first)
            r_ref[side, rows] = first
            p_ref[side, rows] = first
            rho_ref[side, rows] = jnp.broadcast_to(
                jnp.sum(first * first, axis=1, keepdims=True), first.shape
            )

    def step(index, carry):
        for start, stop in chunks:
            rows = slice(start, stop)
            for side in range(2):
                direction = p_ref[side, rows]
                high, rest = two_parts(direction)
                scores = low(within_ref[rows, 0:stop] * dot_nt(high, k_ref[0:stop]))
                image = (
                    decay_ref[rows] * dot_nn(jnp.concatenate([high, rest, high], axis=1), stack_ref[...])
                    + dot_nn(scores, k_ref[0:stop])
                    + ridge * direction
                )
                rho_now = rho_ref[side, rows]
                curve = jnp.sum(direction * image, axis=1, keepdims=True)
                size = rho_now / (curve + epsilon)
                x_ref[side, rows] = x_ref[side, rows] + size * direction
                residual = r_ref[side, rows] - size * image
                r_ref[side, rows] = residual
                rho_next = jnp.sum(residual * residual, axis=1, keepdims=True)
                p_ref[side, rows] = residual + rho_next / (rho_now + epsilon) * direction
                rho_ref[side, rows] = jnp.broadcast_to(rho_next, residual.shape)
        return carry

    lax.fori_loop(0, SOLVE_STEPS, step, 0)
    solved = low(x_ref[0])
    adjoint = low(x_ref[1])
    low_x_ref[...] = solved
    low_y_ref[...] = adjoint
    weighted = low(decay_ref[...] * x_ref[0])
    value_back_ref[0] = dot_tn(g_ref[...], weighted)
    gram_back_ref[0] = -dot_tn(adjoint, weighted)
    for start, stop in chunks:
        rows = slice(start, stop)
        within = within_ref[start:, rows]
        solved_now, adjoint_now, grads = low_x_ref[start:], low_y_ref[start:], g_ref[start:]
        along_solved = low(within * dot_nt(solved_now, k_ref[rows]))
        along_adjoint = low(within * dot_nt(adjoint_now, k_ref[rows]))
        along_values = low(within * dot_nt(grads, v_ref[rows]))
        part_values_ref[rows] = dot_tn(along_solved, grads)
        part_keys_ref[rows] = (
            dot_tn(along_values, solved_now)
            - dot_tn(along_solved, adjoint_now)
            - dot_tn(along_adjoint, solved_now)
        )


def solve_blocks(ridge, log_decay, queries, keys, values, grads_out, gram_start, value_start):
    rows, width = queries.shape
    head_dev = width // DH
    count = rows // SPAN
    units = head_dev * count
    gates = log_decay.reshape(units, 1, SPAN)
    part = pl.BlockSpec((SPAN, DH), lambda u: (u % count, u // count))
    state = pl.BlockSpec((1, DH, DH), lambda u: (u, 0, 0))
    low_shape = jax.ShapeDtypeStruct((rows, width), jnp.bfloat16)
    wide_shape = jax.ShapeDtypeStruct((rows, width), jnp.float32)
    state_shape = jax.ShapeDtypeStruct((units, DH, DH), jnp.float32)
    work = pltpu.VMEM((2, SPAN, DH), jnp.float32)
    return pl.pallas_call(
        functools.partial(solve_kernel, count),
        grid=(units,),
        out_shape=(low_shape, low_shape, wide_shape, wide_shape, state_shape, state_shape),
        in_specs=[
            pl.BlockSpec(memory_space=pltpu.SMEM),
            pl.BlockSpec((1, 1, SPAN), lambda u: (u, 0, 0)),
            part, part, part, part, state, state,
        ],
        out_specs=(part, part, part, part, state, state),
        scratch_shapes=[
            pltpu.VMEM((SPAN, SPAN), jnp.float32),
            pltpu.VMEM((SPAN, DH), jnp.float32),
            pltpu.VMEM((3 * DH, DH), jnp.bfloat16),
            work, work, work, work,
        ],
        compiler_params=pltpu.CompilerParams(vmem_limit_bytes=WORK_BYTES),
        name="solve_blocks",
    )(ridge, gates, queries, keys, values, grads_out, gram_start, value_start)


def split_heads(block, head_dev):
    rows = block.shape[0]
    return block.reshape(rows // SPAN, SPAN, head_dev, DH).transpose(2, 0, 1, 3)


def wide_heads(block):
    head_dev, count, size, width = block.shape
    return block.transpose(1, 2, 0, 3).reshape(count * size, head_dev * width)


def scale_mats(factor, mats):
    return factor[..., None, None] * mats


def shards(queries, keys, values, grads_out, log_decay, ridge):
    gathered = (
        lax.all_to_all(queries, "head", split_axis=1, concat_axis=0, tiled=True),
        lax.all_to_all(keys, "head", split_axis=1, concat_axis=0, tiled=True),
        lax.all_to_all(values, "head", split_axis=1, concat_axis=0, tiled=True),
        lax.all_to_all(grads_out, "head", split_axis=1, concat_axis=0, tiled=True),
    )
    head_dev = log_decay.shape[0]
    query_h = split_heads(gathered[0], head_dev)
    key_h = split_heads(gathered[1], head_dev)
    value_h = split_heads(gathered[2], head_dev)
    grad_h = split_heads(gathered[3], head_dev)
    count = query_h.shape[1]
    gates = log_decay.reshape(head_dev, count, SPAN)
    sums = jnp.sum(gates, axis=2)
    through_local = jnp.cumsum(sums, axis=1)
    starts = jnp.concatenate([jnp.zeros_like(sums[:, :1]), through_local[:, :-1]], axis=1)
    total_log = jnp.sum(sums, axis=1)
    cumul = jnp.cumsum(gates, axis=2)
    key_wide = key_h.astype(jnp.float32)
    scaled_lookup_vectors = jnp.exp(cumul[..., -1:] - cumul)[..., None] * key_wide
    gram_parts = jnp.einsum("hnck,hncl->hnkl", key_wide, scaled_lookup_vectors, precision=highest)
    value_parts = jnp.einsum(
        "hncv,hnck->hnvk", value_h.astype(jnp.float32), scaled_lookup_vectors, precision=highest
    )
    zeros = jnp.zeros((head_dev, DH, DH), jnp.float32)
    gram_carry, value_carry = (zeros, zeros)
    gram_local, value_local = ([], [])
    for block in range(count):
        gram_local.append(gram_carry)
        value_local.append(value_carry)
        decay = jnp.exp(sums[:, block])
        gram_carry = scale_mats(decay, gram_carry) + gram_parts[:, block]
        value_carry = scale_mats(decay, value_carry) + value_parts[:, block]
    position = lax.axis_index("ctx")
    totals = lax.all_gather(total_log[None], "ctx", axis=0, tiled=True)
    through = jnp.cumsum(totals, axis=0)
    exclusive = jnp.concatenate([jnp.zeros_like(totals[:1]), through[:-1]], axis=0)
    mine_excl = lax.dynamic_slice_in_dim(exclusive, position, 1, 0)
    mine_through = lax.dynamic_slice_in_dim(through, position, 1, 0)
    piece = (
        lax.all_gather(gram_carry[None], "ctx", axis=0, tiled=True),
        lax.all_gather(value_carry[None], "ctx", axis=0, tiled=True),
    )
    number = piece[0].shape[0]
    index = jnp.arange(number, dtype=jnp.int32)
    gap = mine_excl - through
    weight = jnp.where((index < position)[:, None], jnp.exp(jnp.minimum(gap, 0.0)), 0.0)
    gram_in = jnp.einsum("jh,jhkl->hkl", weight, piece[0], precision=highest)
    value_in = jnp.einsum("jh,jhkl->hkl", weight, piece[1], precision=highest)
    entry = jnp.exp(starts)
    gram_start = scale_mats(entry, gram_in[:, None]) + jnp.stack(gram_local, axis=1)
    value_start = scale_mats(entry, value_in[:, None]) + jnp.stack(value_local, axis=1)
    units = head_dev * count
    solved, adjoint, part_keys, part_values, value_back, gram_back = solve_blocks(
        ridge,
        log_decay,
        *gathered,
        gram_start.reshape(units, DH, DH),
        value_start.reshape(units, DH, DH),
    )
    value_back = value_back.reshape(head_dev, count, DH, DH)
    gram_back = gram_back.reshape(head_dev, count, DH, DH)
    value_delta = jnp.einsum("hn,hnvk->hvk", entry, value_back, precision=highest)
    gram_delta = jnp.einsum("hn,hnvk->hvk", entry, gram_back, precision=highest)
    piece = (
        lax.all_gather(value_delta[None].astype(jnp.bfloat16), "ctx", axis=0, tiled=True).astype(
            jnp.float32
        ),
        lax.all_gather(gram_delta[None].astype(jnp.bfloat16), "ctx", axis=0, tiled=True).astype(
            jnp.float32
        ),
    )
    number = piece[0].shape[0]
    index = jnp.arange(number, dtype=jnp.int32)
    gap = exclusive - mine_through
    weight = jnp.where((index > position)[:, None], jnp.exp(jnp.minimum(gap, 0.0)), 0.0)
    value_after = zeros + jnp.einsum("jh,jhkl->hkl", weight, piece[0], precision=highest)
    outer_product_suffix = zeros + jnp.einsum("jh,jhkl->hkl", weight, piece[1], precision=highest)
    value_next = [None] * count
    gram_next = [None] * count
    for block in reversed(range(count)):
        value_next[block] = value_after
        gram_next[block] = outer_product_suffix
        decay = jnp.exp(sums[:, block])
        value_after = scale_mats(decay, value_after) + value_back[:, block]
        outer_product_suffix = scale_mats(decay, outer_product_suffix) + gram_back[:, block]
    end_weight = jnp.exp(cumul[..., -1:] - cumul)[..., None]
    value_next = jnp.stack(value_next, axis=1)
    gram_next = jnp.stack(gram_next, axis=1)
    gram_next = low(gram_next + gram_next.swapaxes(2, 3))
    value_next = low(value_next)
    add_values = end_weight * jnp.einsum(
        "hnck,hnvk->hncv", key_h, value_next, preferred_element_type=jnp.float32
    )
    add_keys = end_weight * (
        jnp.einsum("hncv,hnvk->hnck", value_h, value_next, preferred_element_type=jnp.float32)
        + jnp.einsum("hnck,hnkl->hncl", key_h, gram_next, preferred_element_type=jnp.float32)
    )
    grad_keys = low(part_keys + wide_heads(add_keys))
    grad_values = low(part_values + wide_heads(add_values))
    results = (
        lax.all_to_all(adjoint, "head", split_axis=0, concat_axis=1, tiled=True),
        lax.all_to_all(grad_keys, "head", split_axis=0, concat_axis=1, tiled=True),
        lax.all_to_all(grad_values, "head", split_axis=0, concat_axis=1, tiled=True),
    )
    return (results[0], results[1], results[2])


def solution(mesh):
    return jax.shard_map(
        shards,
        mesh=mesh,
        in_specs=(
            P(("ctx", "head"), None),
            P(("ctx", "head"), None),
            P(("ctx", "head"), None),
            P(("ctx", "head"), None),
            P("head", "ctx"),
            P("head"),
        ),
        out_specs=(P(("ctx", "head"), None), P(("ctx", "head"), None), P(("ctx", "head"), None)),
        check_vma=False,
    )
```

```python
import functools

import jax
import jax.numpy as jnp
from jax import lax
from jax.experimental import pallas as pl
from jax.experimental.pallas import tpu as pltpu
from jax.sharding import PartitionSpec as P

DH = 128
SPAN = 512
SOLVE_STEPS = 8


epsilon = 1e-06


CHUNK = 256
WORK_BYTES = 48 * 1024 * 1024


def dot(left, right, dims):
    return lax.dot_general(left, right, (dims, ((), ())), preferred_element_type=jnp.float32)


def dot_nn(left, right):
    return dot(left, right, ((1,), (0,)))


def dot_nt(left, right):
    return dot(left, right, ((1,), (1,)))


def dot_tn(left, right):
    return dot(left, right, ((0,), (0,)))


def low(array):
    return array.astype(jnp.bfloat16)


def two_parts(array):
    high = low(array)
    return high, low(array - high.astype(jnp.float32))


def running_sums(gate_row):
    size = gate_row.shape[1]
    rowpos = lax.broadcasted_iota(jnp.int32, (size, size), 0)
    column_position = lax.broadcasted_iota(jnp.int32, (size, size), 1)
    spread = jnp.broadcast_to(gate_row, (size, size))
    column = jnp.sum(jnp.where(rowpos >= column_position, spread, 0.0), axis=1, keepdims=True)
    gate_column = jnp.sum(jnp.where(rowpos == column_position, spread, 0.0), axis=1, keepdims=True)
    row = jnp.sum(jnp.where(rowpos <= column_position, gate_column, 0.0), axis=0, keepdims=True)
    return column, row, rowpos >= column_position


def solve_kernel(
    count, ridge_ref, gate_ref, q_ref, k_ref, v_ref, g_ref, gram_ref, value_ref,
    low_x_ref, low_y_ref, part_keys_ref, part_values_ref, value_back_ref, gram_back_ref,
    within_ref, decay_ref, stack_ref, x_ref, r_ref, p_ref, rho_ref,
):
    ridge = ridge_ref[pl.program_id(0) // count]
    column, row, causal = running_sums(gate_ref[0])
    within_ref[...] = jnp.where(causal, jnp.exp(jnp.minimum(column - row, 0.0)), 0.0)
    decay_ref[...] = jnp.broadcast_to(jnp.exp(column), decay_ref.shape)
    gram_high, gram_low = two_parts(gram_ref[0])
    stack_ref[0:DH] = gram_high
    stack_ref[DH : 2 * DH] = gram_high
    stack_ref[2 * DH : 3 * DH] = gram_low
    value_high, value_low = two_parts(value_ref[0])
    span = q_ref.shape[0]
    chunks = [(start, start + CHUNK) for start in range(0, span, CHUNK)]
    for start, stop in chunks:
        rows = slice(start, stop)
        grads = g_ref[rows]
        scores = low(within_ref[rows, 0:stop] * dot_nt(grads, v_ref[0:stop]))
        state = dot_nn(grads, value_high) + dot_nn(grads, value_low)
        rhs = decay_ref[rows] * state + dot_nn(scores, k_ref[0:stop])
        for side, first in enumerate((q_ref[rows].astype(jnp.float32), rhs)):
            x_ref[side, rows] = jnp.zeros_like(first)
            r_ref[side, rows] = first
            p_ref[side, rows] = first
            rho_ref[side, rows] = jnp.broadcast_to(
                jnp.sum(first * first, axis=1, keepdims=True), first.shape
            )

    def step(index, carry):
        for start, stop in chunks:
            rows = slice(start, stop)
            for side in range(2):
                direction = p_ref[side, rows]
                high, rest = two_parts(direction)
                scores = low(within_ref[rows, 0:stop] * dot_nt(high, k_ref[0:stop]))
                image = (
                    decay_ref[rows] * dot_nn(jnp.concatenate([high, rest, high], axis=1), stack_ref[...])
                    + dot_nn(scores, k_ref[0:stop])
                    + ridge * direction
                )
                rho_now = rho_ref[side, rows]
                curve = jnp.sum(direction * image, axis=1, keepdims=True)
                size = rho_now / (curve + epsilon)
                x_ref[side, rows] = x_ref[side, rows] + size * direction
                residual = r_ref[side, rows] - size * image
                r_ref[side, rows] = residual
                rho_next = jnp.sum(residual * residual, axis=1, keepdims=True)
                p_ref[side, rows] = residual + rho_next / (rho_now + epsilon) * direction
                rho_ref[side, rows] = jnp.broadcast_to(rho_next, residual.shape)
        return carry

    lax.fori_loop(0, SOLVE_STEPS, step, 0)
    solved = low(x_ref[0])
    adjoint = low(x_ref[1])
    low_x_ref[...] = solved
    low_y_ref[...] = adjoint
    weighted = low(decay_ref[...] * x_ref[0])
    value_back_ref[0] = dot_tn(g_ref[...], weighted)
    gram_back_ref[0] = -dot_tn(adjoint, weighted)
    for start, stop in chunks:
        rows = slice(start, stop)
        within = within_ref[start:, rows]
        solved_now, adjoint_now, grads = low_x_ref[start:], low_y_ref[start:], g_ref[start:]
        along_solved = low(within * dot_nt(solved_now, k_ref[rows]))
        along_adjoint = low(within * dot_nt(adjoint_now, k_ref[rows]))
        along_values = low(within * dot_nt(grads, v_ref[rows]))
        part_values_ref[rows] = dot_tn(along_solved, grads)
        part_keys_ref[rows] = (
            dot_tn(along_values, solved_now)
            - dot_tn(along_solved, adjoint_now)
            - dot_tn(along_adjoint, solved_now)
        )


def solve_blocks(ridge, gates, queries, keys, values, grads_out, gram_start, value_start):
    rows, width = queries.shape
    head_dev = width // DH
    count = rows // SPAN
    units = head_dev * count
    part = pl.BlockSpec((SPAN, DH), lambda u: (u % count, u // count))
    state = pl.BlockSpec((1, DH, DH), lambda u: (u, 0, 0))
    low_shape = jax.ShapeDtypeStruct((rows, width), jnp.bfloat16)
    wide_shape = jax.ShapeDtypeStruct((rows, width), jnp.float32)
    state_shape = jax.ShapeDtypeStruct((units, DH, DH), jnp.float32)
    work = pltpu.VMEM((2, SPAN, DH), jnp.float32)
    return pl.pallas_call(
        functools.partial(solve_kernel, count),
        grid=(units,),
        out_shape=(low_shape, low_shape, wide_shape, wide_shape, state_shape, state_shape),
        in_specs=[
            pl.BlockSpec(memory_space=pltpu.SMEM),
            pl.BlockSpec((1, 1, SPAN), lambda u: (u, 0, 0)),
            part, part, part, part, state, state,
        ],
        out_specs=(part, part, part, part, state, state),
        scratch_shapes=[
            pltpu.VMEM((SPAN, SPAN), jnp.float32),
            pltpu.VMEM((SPAN, DH), jnp.float32),
            pltpu.VMEM((3 * DH, DH), jnp.bfloat16),
            work, work, work, work,
        ],
        compiler_params=pltpu.CompilerParams(vmem_limit_bytes=WORK_BYTES),
        name="solve_blocks",
    )(ridge, gates, queries, keys, values, grads_out, gram_start, value_start)


MESH = pl.DeviceIdType.MESH


def greet(ctx_size, head_size):
    position, lane = lax.axis_index("ctx"), lax.axis_index("head")
    barrier = pltpu.get_barrier_semaphore()
    for offset in range(1, head_size):
        peer = lax.rem(lane + offset, head_size)
        pl.semaphore_signal(barrier, inc=1, device_id=(position, peer), device_id_type=MESH)
    for offset in range(1, ctx_size):
        peer = lax.rem(position + offset, ctx_size)
        pl.semaphore_signal(barrier, inc=1, device_id=(peer, lane), device_id_type=MESH)
    pl.semaphore_wait(barrier, head_size + ctx_size - 2)


def end_weights(gate_row):
    size = gate_row.shape[1]
    rowpos = lax.broadcasted_iota(jnp.int32, (size, size), 0)
    column_position = lax.broadcasted_iota(jnp.int32, (size, size), 1)
    spread = jnp.broadcast_to(gate_row, (size, size))
    return jnp.exp(jnp.sum(jnp.where(column_position > rowpos, spread, 0.0), axis=1, keepdims=True))


def log_between(totals, first, stop):
    gathered = jnp.zeros_like(totals[0])
    for index, tile in enumerate(totals):
        gathered = gathered + jnp.where(
            jnp.logical_and(index >= first, index < stop), tile, jnp.zeros_like(tile)
        )
    return gathered


def scale_heads(tile, mats, head_dev):
    return [jnp.exp(tile[u // 2 : u // 2 + 1]) * mats[u] for u in range(2 * head_dev)]


def doubling(reverse, ctx_size, head_dev, totals, mats, send_ref, slot_ref, send_sem, recv_sem):
    position, lane = lax.axis_index("ctx"), lax.axis_index("head")
    outside = [jnp.zeros((DH, DH), jnp.float32) for _ in mats]
    size, turn = 1, 0
    while size < ctx_size:
        late = lax.rem(position // size, 2)
        partner = position + size * (1 - 2 * late)
        for u, mat in enumerate(mats):
            send_ref[turn, u] = low(mat)
        copy = pltpu.make_async_remote_copy(
            src_ref=send_ref.at[turn],
            dst_ref=slot_ref.at[turn],
            send_sem=send_sem.at[turn],
            recv_sem=recv_sem.at[turn],
            device_id=(partner, lane),
            device_id_type=MESH,
        )
        copy.start()
        first = position - lax.rem(position, size)
        other = first + size * (1 - 2 * late)
        if reverse:
            takes = late == 0
            gap = log_between(totals, position + 1, first + size)
        else:
            takes = late == 1
            gap = log_between(totals, first, position)
        own_log = log_between(totals, first, first + size)
        other_log = log_between(totals, other, other + size)
        zero_log = jnp.zeros_like(own_log)
        theirs_log = jnp.where(takes, own_log, zero_log)
        mine_log = jnp.where(takes, zero_log, other_log)
        share = jnp.where(takes, 1.0, 0.0)
        copy.wait()
        theirs = [slot_ref[turn, u].astype(jnp.float32) for u in range(2 * head_dev)]
        gapped = scale_heads(gap, theirs, head_dev)
        outside = [kept + share * more for kept, more in zip(outside, gapped)]
        mats = [
            one + two
            for one, two in zip(
                scale_heads(theirs_log, theirs, head_dev), scale_heads(mine_log, mats, head_dev)
            )
        ]
        size, turn = 2 * size, turn + 1
    return outside


def exchange_kernel(
    ctx_size, head_size, gate_ref, k_in, v_in, q_in, g_in,
    k_ref, v_ref, q_ref, g_ref, gram_ref, value_ref, totals_ref,
    send_ref, slot_ref, own_sem, part_send, part_recv, total_send, total_recv, scan_send, scan_recv,
):
    position, lane = lax.axis_index("ctx"), lax.axis_index("head")
    rows, width = k_in.shape[0], k_ref.shape[1]
    units = gate_ref.shape[0]
    head_dev = width // DH
    count = units // head_dev
    greet(ctx_size, head_size)
    copies = {}
    for index, (source, target) in enumerate(((k_in, k_ref), (v_in, v_ref), (q_in, q_ref), (g_in, g_ref))):
        place = target.at[pl.ds(pl.multiple_of(lane * rows, rows), rows)]
        for offset in range(1, head_size):
            peer = lax.rem(lane + offset, head_size)
            copies[index, offset] = pltpu.make_async_remote_copy(
                src_ref=source.at[:, pl.ds(pl.multiple_of(peer * width, width), width)],
                dst_ref=place,
                send_sem=part_send.at[index, offset - 1],
                recv_sem=part_recv.at[index, offset - 1],
                device_id=(position, peer),
                device_id_type=MESH,
            )
            copies[index, offset].start()
        copies[index, 0] = pltpu.make_async_copy(
            source.at[:, pl.ds(pl.multiple_of(lane * width, width), width)], place, own_sem.at[index]
        )
        copies[index, 0].start()
    sums = [jnp.sum(gate_ref[u], axis=1, keepdims=True) for u in range(units)]
    heads = []
    for head in range(head_dev):
        total = sums[head * count]
        for block in range(1, count):
            total = total + sums[head * count + block]
        heads.append(jnp.broadcast_to(total, (1, DH)))
    heads.append(jnp.zeros((8 - head_dev, DH), jnp.float32))
    totals_ref[position] = jnp.concatenate(heads, axis=0)
    total_copies = []
    for offset in range(1, ctx_size):
        peer = lax.rem(position + offset, ctx_size)
        copy = pltpu.make_async_remote_copy(
            src_ref=totals_ref.at[position],
            dst_ref=totals_ref.at[position],
            send_sem=total_send.at[offset - 1],
            recv_sem=total_recv.at[offset - 1],
            device_id=(peer, lane),
            device_id_type=MESH,
        )
        copy.start()
        total_copies.append(copy)
    weights = [end_weights(gate_ref[u]) for u in range(units)]
    for index in (0, 1):
        copies[index, 0].wait()
        for offset in range(1, head_size):
            copies[index, offset].wait()
    mats, starts = [], []
    for head in range(head_dev):
        columns = slice(head * DH, (head + 1) * DH)
        pair = None
        for block in range(count):
            u = head * count + block
            span = slice(block * SPAN, (block + 1) * SPAN)
            keys = k_ref[span, columns]
            weighted = low(weights[u] * keys.astype(jnp.float32))
            made = (dot_tn(keys, weighted), dot_tn(v_ref[span, columns], weighted))
            if pair is None:
                pair, passed = made, sums[u]
            else:
                gram_ref[u], value_ref[u] = pair
                starts.append((u, head, passed))
                decay = jnp.exp(sums[u])
                pair = tuple(decay * old + new for old, new in zip(pair, made))
                passed = passed + sums[u]
        mats.extend(pair)
    for copy in total_copies:
        copy.wait()
    totals = [totals_ref[index] for index in range(ctx_size)]
    before = doubling(
        False, ctx_size, head_dev, totals, mats, send_ref, slot_ref, scan_send, scan_recv
    )
    for head in range(head_dev):
        gram_ref[head * count] = before[2 * head]
        value_ref[head * count] = before[2 * head + 1]
    for u, head, passed in starts:
        decay = jnp.exp(passed)
        gram_ref[u] = gram_ref[u] + decay * before[2 * head]
        value_ref[u] = value_ref[u] + decay * before[2 * head + 1]
    for index in (2, 3):
        copies[index, 0].wait()
        for offset in range(1, head_size):
            copies[index, offset].wait()


def rounds_of(ctx_size):
    return (ctx_size - 1).bit_length()


def exchange(ctx_size, head_size, gates, queries, keys, values, grads_out):
    rows, columns = queries.shape
    width = columns // head_size
    units = gates.shape[0]
    head_dev = width // DH
    rounds = rounds_of(ctx_size)
    vmem = pl.BlockSpec(memory_space=pltpu.VMEM)
    part = jax.ShapeDtypeStruct((rows * head_size, width), jnp.bfloat16)
    state = jax.ShapeDtypeStruct((units, DH, DH), jnp.float32)
    return pl.pallas_call(
        functools.partial(exchange_kernel, ctx_size, head_size),
        out_shape=(part, part, part, part, state, state, jax.ShapeDtypeStruct((ctx_size, 8, DH), jnp.float32)),
        in_specs=[vmem] * 5,
        out_specs=(vmem,) * 7,
        scratch_shapes=[
            pltpu.VMEM((rounds, 2 * head_dev, DH, DH), jnp.bfloat16),
            pltpu.VMEM((rounds, 2 * head_dev, DH, DH), jnp.bfloat16),
            pltpu.SemaphoreType.DMA((4,)),
            pltpu.SemaphoreType.DMA((4, head_size - 1)),
            pltpu.SemaphoreType.DMA((4, head_size - 1)),
            pltpu.SemaphoreType.DMA((ctx_size - 1,)),
            pltpu.SemaphoreType.DMA((ctx_size - 1,)),
            pltpu.SemaphoreType.DMA((rounds,)),
            pltpu.SemaphoreType.DMA((rounds,)),
        ],
        compiler_params=pltpu.CompilerParams(
            collective_id=0, has_side_effects=True, vmem_limit_bytes=WORK_BYTES
        ),
        name="exchange",
    )(gates, keys, values, queries, grads_out)


def finish_kernel(
    ctx_size, head_size, gate_ref, totals_ref, value_back_ref, gram_back_ref,
    part_keys_ref, part_values_ref, k_ref, v_ref, adjoint_ref,
    query_out, key_out, value_out,
    keys_ready, values_ready, send_ref, slot_ref, own_sem, part_send, part_recv, scan_send, scan_recv,
):
    position, lane = lax.axis_index("ctx"), lax.axis_index("head")
    rows, width = query_out.shape[0], k_ref.shape[1]
    units = gate_ref.shape[0]
    head_dev = width // DH
    count = units // head_dev
    greet(ctx_size, head_size)
    copies = []

    def send_back(index, source, target):
        place = target.at[:, pl.ds(pl.multiple_of(lane * width, width), width)]
        for offset in range(1, head_size):
            peer = lax.rem(lane + offset, head_size)
            copies.append(
                pltpu.make_async_remote_copy(
                    src_ref=source.at[pl.ds(pl.multiple_of(peer * rows, rows), rows)],
                    dst_ref=place,
                    send_sem=part_send.at[index, offset - 1],
                    recv_sem=part_recv.at[index, offset - 1],
                    device_id=(position, peer),
                    device_id_type=MESH,
                )
            )
            copies[-1].start()
        copies.append(
            pltpu.make_async_copy(
                source.at[pl.ds(pl.multiple_of(lane * rows, rows), rows)], place, own_sem.at[index]
            )
        )
        copies[-1].start()

    sums = [jnp.sum(gate_ref[u], axis=1, keepdims=True) for u in range(units)]
    mats = []
    for head in range(head_dev):
        last = head * count + count - 1
        pair = (value_back_ref[last], gram_back_ref[last])
        for block in reversed(range(count - 1)):
            u = head * count + block
            decay = jnp.exp(sums[u])
            pair = (decay * pair[0] + value_back_ref[u], decay * pair[1] + gram_back_ref[u])
        mats.extend(pair)
    totals = [totals_ref[index] for index in range(ctx_size)]
    after = doubling(
        True, ctx_size, head_dev, totals, mats, send_ref, slot_ref, scan_send, scan_recv
    )
    send_back(0, adjoint_ref, query_out)
    for head in range(head_dev):
        columns = slice(head * DH, (head + 1) * DH)
        value_next, gram_next = after[2 * head], after[2 * head + 1]
        for block in reversed(range(count)):
            u = head * count + block
            span = slice(block * SPAN, (block + 1) * SPAN)
            weight = end_weights(gate_ref[u])
            value_low = low(value_next)
            gram_low = low(gram_next + gram_next.T)
            keys, values = k_ref[span, columns], v_ref[span, columns]
            values_ready[span, columns] = low(
                part_values_ref[span, columns] + weight * dot_nt(keys, value_low)
            )
            keys_ready[span, columns] = low(
                part_keys_ref[span, columns]
                + weight * (dot_nn(values, value_low) + dot_nn(keys, gram_low))
            )
            decay = jnp.exp(sums[u])
            value_next = decay * value_next + value_back_ref[u]
            gram_next = decay * gram_next + gram_back_ref[u]
    send_back(1, keys_ready, key_out)
    send_back(2, values_ready, value_out)
    for copy in copies:
        copy.wait()


def finish(ctx_size, head_size, gates, totals, value_back, gram_back, part_keys, part_values, keys, values, adjoint):
    length, width = keys.shape
    rows = length // head_size
    head_dev = width // DH
    rounds = rounds_of(ctx_size)
    vmem = pl.BlockSpec(memory_space=pltpu.VMEM)
    out = jax.ShapeDtypeStruct((rows, width * head_size), jnp.bfloat16)
    return pl.pallas_call(
        functools.partial(finish_kernel, ctx_size, head_size),
        out_shape=(out, out, out),
        in_specs=[vmem] * 9,
        out_specs=(vmem,) * 3,
        scratch_shapes=[
            pltpu.VMEM((length, width), jnp.bfloat16),
            pltpu.VMEM((length, width), jnp.bfloat16),
            pltpu.VMEM((rounds, 2 * head_dev, DH, DH), jnp.bfloat16),
            pltpu.VMEM((rounds, 2 * head_dev, DH, DH), jnp.bfloat16),
            pltpu.SemaphoreType.DMA((3,)),
            pltpu.SemaphoreType.DMA((3, head_size - 1)),
            pltpu.SemaphoreType.DMA((3, head_size - 1)),
            pltpu.SemaphoreType.DMA((rounds,)),
            pltpu.SemaphoreType.DMA((rounds,)),
        ],
        compiler_params=pltpu.CompilerParams(
            collective_id=1, has_side_effects=True, vmem_limit_bytes=WORK_BYTES
        ),
        name="finish",
    )(gates, totals, value_back, gram_back, part_keys, part_values, keys, values, adjoint)


def shards(ctx_size, head_size, queries, keys, values, grads_out, log_decay, ridge):
    gates = log_decay.reshape(-1, 1, SPAN)
    keys, values, queries, grads_out, gram_start, value_start, totals = exchange(
        ctx_size, head_size, gates, queries, keys, values, grads_out
    )
    solved, adjoint, part_keys, part_values, value_back, gram_back = solve_blocks(
        ridge, gates, queries, keys, values, grads_out, gram_start, value_start
    )
    return finish(
        ctx_size, head_size, gates, totals, value_back, gram_back, part_keys, part_values, keys, values, adjoint
    )


def solution(mesh):
    return jax.shard_map(
        functools.partial(shards, mesh.shape["ctx"], mesh.shape["head"]),
        mesh=mesh,
        in_specs=(
            P(("ctx", "head"), None),
            P(("ctx", "head"), None),
            P(("ctx", "head"), None),
            P(("ctx", "head"), None),
            P("head", "ctx"),
            P("head"),
        ),
        out_specs=(P(("ctx", "head"), None), P(("ctx", "head"), None), P(("ctx", "head"), None)),
        check_vma=False,
    )
```

```python
import functools

import jax
import jax.numpy as jnp
from jax import lax
from jax.experimental import pallas as pl
from jax.experimental.pallas import tpu as pltpu
from jax.sharding import PartitionSpec as P

DH = 128
SPAN = 512
SOLVE_STEPS = 8


epsilon = 1e-06


CHUNK = 256
WORK_BYTES = 48 * 1024 * 1024


def dot(left, right, dims):
    return lax.dot_general(left, right, (dims, ((), ())), preferred_element_type=jnp.float32)


def dot_nn(left, right):
    return dot(left, right, ((1,), (0,)))


def dot_nt(left, right):
    return dot(left, right, ((1,), (1,)))


def dot_tn(left, right):
    return dot(left, right, ((0,), (0,)))


def low(array):
    return array.astype(jnp.bfloat16)


def two_parts(array):
    high = low(array)
    return high, low(array - high.astype(jnp.float32))


def running_sums(gate_row):
    size = gate_row.shape[1]
    rowpos = lax.broadcasted_iota(jnp.int32, (size, size), 0)
    column_position = lax.broadcasted_iota(jnp.int32, (size, size), 1)
    spread = jnp.broadcast_to(gate_row, (size, size))
    column = jnp.sum(jnp.where(rowpos >= column_position, spread, 0.0), axis=1, keepdims=True)
    gate_column = jnp.sum(jnp.where(rowpos == column_position, spread, 0.0), axis=1, keepdims=True)
    row = jnp.sum(jnp.where(rowpos <= column_position, gate_column, 0.0), axis=0, keepdims=True)
    return column, row, rowpos >= column_position


def solve_kernel(
    count, ridge_ref, gate_ref, q_ref, k_ref, v_ref, g_ref, gram_ref, value_ref,
    low_x_ref, low_y_ref, part_keys_ref, part_values_ref, value_back_ref, gram_back_ref,
    within_ref, decay_ref, stack_ref, x_ref, r_ref, p_ref, rho_ref,
):
    ridge = ridge_ref[pl.program_id(0) // count]
    column, row, causal = running_sums(gate_ref[0])
    within_ref[...] = jnp.where(causal, jnp.exp(jnp.minimum(column - row, 0.0)), 0.0)
    decay_ref[...] = jnp.broadcast_to(jnp.exp(column), decay_ref.shape)
    gram_high, gram_low = two_parts(gram_ref[0])
    stack_ref[0:DH] = gram_high
    stack_ref[DH : 2 * DH] = gram_low
    value_high, value_low = two_parts(value_ref[0])
    span = q_ref.shape[0]
    chunks = [(start, start + CHUNK) for start in range(0, span, CHUNK)]
    for start, stop in chunks:
        rows = slice(start, stop)
        grads = g_ref[rows]
        scores = low(within_ref[rows, 0:stop] * dot_nt(grads, v_ref[0:stop]))
        state = dot_nn(grads, value_high) + dot_nn(grads, value_low)
        rhs = decay_ref[rows] * state + dot_nn(scores, k_ref[0:stop])
        for side, first in enumerate((q_ref[rows].astype(jnp.float32), rhs)):
            x_ref[side, rows] = jnp.zeros_like(first)
            r_ref[side, rows] = first
            p_ref[side, rows] = first
            rho_ref[side, rows] = jnp.broadcast_to(
                jnp.sum(first * first, axis=1, keepdims=True), first.shape
            )

    def step(index, carry):
        for start, stop in chunks:
            rows = slice(start, stop)
            for side in range(2):
                direction = p_ref[side, rows]
                high = low(direction)
                scores = low(within_ref[rows, 0:stop] * dot_nt(high, k_ref[0:stop]))
                image = (
                    decay_ref[rows] * dot_nn(jnp.concatenate([high, high], axis=1), stack_ref[...])
                    + dot_nn(scores, k_ref[0:stop])
                    + ridge * direction
                )
                rho_now = rho_ref[side, rows]
                curve = jnp.sum(direction * image, axis=1, keepdims=True)
                size = rho_now / (curve + epsilon)
                x_ref[side, rows] = x_ref[side, rows] + size * direction
                residual = r_ref[side, rows] - size * image
                r_ref[side, rows] = residual
                rho_next = jnp.sum(residual * residual, axis=1, keepdims=True)
                p_ref[side, rows] = residual + rho_next / (rho_now + epsilon) * direction
                rho_ref[side, rows] = jnp.broadcast_to(rho_next, residual.shape)
        return carry

    lax.fori_loop(0, SOLVE_STEPS, step, 0)
    solved = low(x_ref[0])
    adjoint = low(x_ref[1])
    low_x_ref[...] = solved
    low_y_ref[...] = adjoint
    weighted = low(decay_ref[...] * x_ref[0])
    value_back_ref[0] = dot_tn(g_ref[...], weighted)
    gram_back_ref[0] = -dot_tn(adjoint, weighted)
    for start, stop in chunks:
        rows = slice(start, stop)
        within = within_ref[start:, rows]
        solved_now, adjoint_now, grads = low_x_ref[start:], low_y_ref[start:], g_ref[start:]
        along_solved = low(within * dot_nt(solved_now, k_ref[rows]))
        along_adjoint = low(within * dot_nt(adjoint_now, k_ref[rows]))
        along_values = low(within * dot_nt(grads, v_ref[rows]))
        part_values_ref[rows] = dot_tn(along_solved, grads)
        part_keys_ref[rows] = (
            dot_tn(along_values, solved_now)
            - dot_tn(along_solved, adjoint_now)
            - dot_tn(along_adjoint, solved_now)
        )


def solve_blocks(ridge, gates, queries, keys, values, grads_out, gram_start, value_start):
    rows, width = queries.shape
    head_dev = width // DH
    count = rows // SPAN
    units = head_dev * count
    part = pl.BlockSpec((SPAN, DH), lambda u: (u % count, u // count))
    state = pl.BlockSpec((1, DH, DH), lambda u: (u, 0, 0))
    low_shape = jax.ShapeDtypeStruct((rows, width), jnp.bfloat16)
    wide_shape = jax.ShapeDtypeStruct((rows, width), jnp.float32)
    state_shape = jax.ShapeDtypeStruct((units, DH, DH), jnp.float32)
    work = pltpu.VMEM((2, SPAN, DH), jnp.float32)
    return pl.pallas_call(
        functools.partial(solve_kernel, count),
        grid=(units,),
        out_shape=(low_shape, low_shape, wide_shape, wide_shape, state_shape, state_shape),
        in_specs=[
            pl.BlockSpec(memory_space=pltpu.SMEM),
            pl.BlockSpec((1, 1, SPAN), lambda u: (u, 0, 0)),
            part, part, part, part, state, state,
        ],
        out_specs=(part, part, part, part, state, state),
        scratch_shapes=[
            pltpu.VMEM((SPAN, SPAN), jnp.float32),
            pltpu.VMEM((SPAN, DH), jnp.float32),
            pltpu.VMEM((2 * DH, DH), jnp.bfloat16),
            work, work, work, work,
        ],
        compiler_params=pltpu.CompilerParams(vmem_limit_bytes=WORK_BYTES),
        name="solve_blocks",
    )(ridge, gates, queries, keys, values, grads_out, gram_start, value_start)


MESH = pl.DeviceIdType.MESH


def greet(ctx_size, head_size):
    position, lane = lax.axis_index("ctx"), lax.axis_index("head")
    barrier = pltpu.get_barrier_semaphore()
    for offset in range(1, head_size):
        peer = lax.rem(lane + offset, head_size)
        pl.semaphore_signal(barrier, inc=1, device_id=(position, peer), device_id_type=MESH)
    for offset in range(1, ctx_size):
        peer = lax.rem(position + offset, ctx_size)
        pl.semaphore_signal(barrier, inc=1, device_id=(peer, lane), device_id_type=MESH)
    pl.semaphore_wait(barrier, head_size + ctx_size - 2)


def end_weights(gate_row):
    size = gate_row.shape[1]
    rowpos = lax.broadcasted_iota(jnp.int32, (size, size), 0)
    column_position = lax.broadcasted_iota(jnp.int32, (size, size), 1)
    spread = jnp.broadcast_to(gate_row, (size, size))
    return jnp.exp(jnp.sum(jnp.where(column_position > rowpos, spread, 0.0), axis=1, keepdims=True))


def log_between(totals, first, stop):
    gathered = jnp.zeros_like(totals[0])
    for index, tile in enumerate(totals):
        gathered = gathered + jnp.where(
            jnp.logical_and(index >= first, index < stop), tile, jnp.zeros_like(tile)
        )
    return gathered


def scale_heads(tile, mats, head_dev):
    return [jnp.exp(tile[u // 2 : u // 2 + 1]) * mats[u] for u in range(2 * head_dev)]


def doubling(
    reverse, ctx_size, head_dev, totals, mats, send_ref, slot_ref, send_sem, recv_sem, meanwhile=None
):
    position, lane = lax.axis_index("ctx"), lax.axis_index("head")
    outside = [jnp.zeros((DH, DH), jnp.float32) for _ in mats]
    size, turn = 1, 0
    while size < ctx_size:
        late = lax.rem(position // size, 2)
        partner = position + size * (1 - 2 * late)
        for u, mat in enumerate(mats):
            send_ref[turn, u] = low(mat)
        copy = pltpu.make_async_remote_copy(
            src_ref=send_ref.at[turn],
            dst_ref=slot_ref.at[turn],
            send_sem=send_sem.at[turn],
            recv_sem=recv_sem.at[turn],
            device_id=(partner, lane),
            device_id_type=MESH,
        )
        copy.start()
        first = position - lax.rem(position, size)
        other = first + size * (1 - 2 * late)
        if reverse:
            takes = late == 0
            gap = log_between(totals, position + 1, first + size)
        else:
            takes = late == 1
            gap = log_between(totals, first, position)
        own_log = log_between(totals, first, first + size)
        other_log = log_between(totals, other, other + size)
        zero_log = jnp.zeros_like(own_log)
        theirs_log = jnp.where(takes, own_log, zero_log)
        mine_log = jnp.where(takes, zero_log, other_log)
        share = jnp.where(takes, 1.0, 0.0)
        if meanwhile is not None and turn == 0:
            meanwhile()
        copy.wait()
        theirs = [slot_ref[turn, u].astype(jnp.float32) for u in range(2 * head_dev)]
        gapped = scale_heads(gap, theirs, head_dev)
        outside = [kept + share * more for kept, more in zip(outside, gapped)]
        mats = [
            one + two
            for one, two in zip(
                scale_heads(theirs_log, theirs, head_dev), scale_heads(mine_log, mats, head_dev)
            )
        ]
        size, turn = 2 * size, turn + 1
    return outside


def exchange_kernel(
    ctx_size, head_size, gate_ref, k_in, v_in, q_in, g_in,
    k_ref, v_ref, q_ref, g_ref, gram_ref, value_ref, totals_ref,
    send_ref, slot_ref, own_sem, part_send, part_recv, total_send, total_recv, scan_send, scan_recv,
):
    position, lane = lax.axis_index("ctx"), lax.axis_index("head")
    rows, width = k_in.shape[0], k_ref.shape[1]
    units = gate_ref.shape[0]
    head_dev = width // DH
    count = units // head_dev
    greet(ctx_size, head_size)
    copies = {}
    for index, (source, target) in enumerate(((k_in, k_ref), (v_in, v_ref), (q_in, q_ref), (g_in, g_ref))):
        place = target.at[pl.ds(pl.multiple_of(lane * rows, rows), rows)]
        for offset in range(1, head_size):
            peer = lax.rem(lane + offset, head_size)
            copies[index, offset] = pltpu.make_async_remote_copy(
                src_ref=source.at[:, pl.ds(pl.multiple_of(peer * width, width), width)],
                dst_ref=place,
                send_sem=part_send.at[index, offset - 1],
                recv_sem=part_recv.at[index, offset - 1],
                device_id=(position, peer),
                device_id_type=MESH,
            )
            copies[index, offset].start()
        copies[index, 0] = pltpu.make_async_copy(
            source.at[:, pl.ds(pl.multiple_of(lane * width, width), width)], place, own_sem.at[index]
        )
        copies[index, 0].start()
    sums = [jnp.sum(gate_ref[u], axis=1, keepdims=True) for u in range(units)]
    heads = []
    for head in range(head_dev):
        total = sums[head * count]
        for block in range(1, count):
            total = total + sums[head * count + block]
        heads.append(jnp.broadcast_to(total, (1, DH)))
    heads.append(jnp.zeros((8 - head_dev, DH), jnp.float32))
    totals_ref[position] = jnp.concatenate(heads, axis=0)
    total_copies = []
    for offset in range(1, ctx_size):
        peer = lax.rem(position + offset, ctx_size)
        copy = pltpu.make_async_remote_copy(
            src_ref=totals_ref.at[position],
            dst_ref=totals_ref.at[position],
            send_sem=total_send.at[offset - 1],
            recv_sem=total_recv.at[offset - 1],
            device_id=(peer, lane),
            device_id_type=MESH,
        )
        copy.start()
        total_copies.append(copy)
    weights = [end_weights(gate_ref[u]) for u in range(units)]
    for index in (0, 1):
        copies[index, 0].wait()
        for offset in range(1, head_size):
            copies[index, offset].wait()
    mats, starts = [], []
    for head in range(head_dev):
        columns = slice(head * DH, (head + 1) * DH)
        pair = None
        for block in range(count):
            u = head * count + block
            span = slice(block * SPAN, (block + 1) * SPAN)
            keys = k_ref[span, columns]
            weighted = low(weights[u] * keys.astype(jnp.float32))
            made = (dot_tn(keys, weighted), dot_tn(v_ref[span, columns], weighted))
            if pair is None:
                pair, passed = made, sums[u]
            else:
                gram_ref[u], value_ref[u] = pair
                starts.append((u, head, passed))
                decay = jnp.exp(sums[u])
                pair = tuple(decay * old + new for old, new in zip(pair, made))
                passed = passed + sums[u]
        mats.extend(pair)
    for copy in total_copies:
        copy.wait()
    totals = [totals_ref[index] for index in range(ctx_size)]
    before = doubling(
        False, ctx_size, head_dev, totals, mats, send_ref, slot_ref, scan_send, scan_recv
    )
    for head in range(head_dev):
        gram_ref[head * count] = before[2 * head]
        value_ref[head * count] = before[2 * head + 1]
    for u, head, passed in starts:
        decay = jnp.exp(passed)
        gram_ref[u] = gram_ref[u] + decay * before[2 * head]
        value_ref[u] = value_ref[u] + decay * before[2 * head + 1]
    for index in (2, 3):
        copies[index, 0].wait()
        for offset in range(1, head_size):
            copies[index, offset].wait()


def rounds_of(ctx_size):
    return (ctx_size - 1).bit_length()


def exchange(ctx_size, head_size, gates, queries, keys, values, grads_out):
    rows, columns = queries.shape
    width = columns // head_size
    units = gates.shape[0]
    head_dev = width // DH
    rounds = rounds_of(ctx_size)
    vmem = pl.BlockSpec(memory_space=pltpu.VMEM)
    part = jax.ShapeDtypeStruct((rows * head_size, width), jnp.bfloat16)
    state = jax.ShapeDtypeStruct((units, DH, DH), jnp.float32)
    return pl.pallas_call(
        functools.partial(exchange_kernel, ctx_size, head_size),
        out_shape=(part, part, part, part, state, state, jax.ShapeDtypeStruct((ctx_size, 8, DH), jnp.float32)),
        in_specs=[vmem] + [pl.BlockSpec(memory_space=pl.ANY)] * 4,
        out_specs=(vmem,) * 7,
        scratch_shapes=[
            pltpu.VMEM((rounds, 2 * head_dev, DH, DH), jnp.bfloat16),
            pltpu.VMEM((rounds, 2 * head_dev, DH, DH), jnp.bfloat16),
            pltpu.SemaphoreType.DMA((4,)),
            pltpu.SemaphoreType.DMA((4, head_size - 1)),
            pltpu.SemaphoreType.DMA((4, head_size - 1)),
            pltpu.SemaphoreType.DMA((ctx_size - 1,)),
            pltpu.SemaphoreType.DMA((ctx_size - 1,)),
            pltpu.SemaphoreType.DMA((rounds,)),
            pltpu.SemaphoreType.DMA((rounds,)),
        ],
        compiler_params=pltpu.CompilerParams(
            collective_id=0, has_side_effects=True, vmem_limit_bytes=WORK_BYTES
        ),
        name="exchange",
    )(gates, keys, values, queries, grads_out)


def finish_kernel(
    ctx_size, head_size, gate_ref, totals_ref, value_back_ref, gram_back_ref,
    part_keys_ref, part_values_ref, k_ref, v_ref, adjoint_ref,
    query_out, key_out, value_out,
    keys_ready, values_ready, send_ref, slot_ref, own_sem, part_send, part_recv, scan_send, scan_recv,
):
    position, lane = lax.axis_index("ctx"), lax.axis_index("head")
    rows, width = query_out.shape[0], k_ref.shape[1]
    units = gate_ref.shape[0]
    head_dev = width // DH
    count = units // head_dev
    greet(ctx_size, head_size)
    copies = []

    def send_back(index, source, target):
        place = target.at[:, pl.ds(pl.multiple_of(lane * width, width), width)]
        for offset in range(1, head_size):
            peer = lax.rem(lane + offset, head_size)
            copies.append(
                pltpu.make_async_remote_copy(
                    src_ref=source.at[pl.ds(pl.multiple_of(peer * rows, rows), rows)],
                    dst_ref=place,
                    send_sem=part_send.at[index, offset - 1],
                    recv_sem=part_recv.at[index, offset - 1],
                    device_id=(position, peer),
                    device_id_type=MESH,
                )
            )
            copies[-1].start()
        copies.append(
            pltpu.make_async_copy(
                source.at[pl.ds(pl.multiple_of(lane * rows, rows), rows)], place, own_sem.at[index]
            )
        )
        copies[-1].start()

    sums = [jnp.sum(gate_ref[u], axis=1, keepdims=True) for u in range(units)]
    mats = []
    for head in range(head_dev):
        last = head * count + count - 1
        pair = (value_back_ref[last], gram_back_ref[last])
        for block in reversed(range(count - 1)):
            u = head * count + block
            decay = jnp.exp(sums[u])
            pair = (decay * pair[0] + value_back_ref[u], decay * pair[1] + gram_back_ref[u])
        mats.extend(pair)
    totals = [totals_ref[index] for index in range(ctx_size)]
    weights = []

    def meanwhile():
        send_back(0, adjoint_ref, query_out)
        weights.extend(end_weights(gate_ref[u]) for u in range(units))

    after = doubling(
        True, ctx_size, head_dev, totals, mats, send_ref, slot_ref, scan_send, scan_recv, meanwhile
    )
    states = []
    for head in range(head_dev):
        columns = slice(head * DH, (head + 1) * DH)
        value_next, gram_next = after[2 * head], after[2 * head + 1]
        for block in reversed(range(count)):
            u = head * count + block
            span = slice(block * SPAN, (block + 1) * SPAN)
            value_low = low(value_next)
            values_ready[span, columns] = low(
                part_values_ref[span, columns] + weights[u] * dot_nt(k_ref[span, columns], value_low)
            )
            states.append((u, span, columns, value_low, low(gram_next + gram_next.T)))
            decay = jnp.exp(sums[u])
            value_next = decay * value_next + value_back_ref[u]
            gram_next = decay * gram_next + gram_back_ref[u]
    send_back(1, values_ready, value_out)
    for u, span, columns, value_low, gram_low in states:
        added = dot_nn(v_ref[span, columns], value_low) + dot_nn(k_ref[span, columns], gram_low)
        keys_ready[span, columns] = low(part_keys_ref[span, columns] + weights[u] * added)
    send_back(2, keys_ready, key_out)
    for copy in copies:
        copy.wait()


def finish(ctx_size, head_size, gates, totals, value_back, gram_back, part_keys, part_values, keys, values, adjoint):
    length, width = keys.shape
    rows = length // head_size
    head_dev = width // DH
    rounds = rounds_of(ctx_size)
    vmem = pl.BlockSpec(memory_space=pltpu.VMEM)
    out = jax.ShapeDtypeStruct((rows, width * head_size), jnp.bfloat16)
    return pl.pallas_call(
        functools.partial(finish_kernel, ctx_size, head_size),
        out_shape=(out, out, out),
        in_specs=[vmem] * 9,
        out_specs=(vmem,) * 3,
        scratch_shapes=[
            pltpu.VMEM((length, width), jnp.bfloat16),
            pltpu.VMEM((length, width), jnp.bfloat16),
            pltpu.VMEM((rounds, 2 * head_dev, DH, DH), jnp.bfloat16),
            pltpu.VMEM((rounds, 2 * head_dev, DH, DH), jnp.bfloat16),
            pltpu.SemaphoreType.DMA((3,)),
            pltpu.SemaphoreType.DMA((3, head_size - 1)),
            pltpu.SemaphoreType.DMA((3, head_size - 1)),
            pltpu.SemaphoreType.DMA((rounds,)),
            pltpu.SemaphoreType.DMA((rounds,)),
        ],
        compiler_params=pltpu.CompilerParams(
            collective_id=1, has_side_effects=True, vmem_limit_bytes=WORK_BYTES
        ),
        name="finish",
    )(gates, totals, value_back, gram_back, part_keys, part_values, keys, values, adjoint)


def shards(ctx_size, head_size, queries, keys, values, grads_out, log_decay, ridge):
    gates = log_decay.reshape(-1, 1, SPAN)
    keys, values, queries, grads_out, gram_start, value_start, totals = exchange(
        ctx_size, head_size, gates, queries, keys, values, grads_out
    )
    solved, adjoint, part_keys, part_values, value_back, gram_back = solve_blocks(
        ridge, gates, queries, keys, values, grads_out, gram_start, value_start
    )
    return finish(
        ctx_size, head_size, gates, totals, value_back, gram_back, part_keys, part_values, keys, values, adjoint
    )


def solution(mesh):
    return jax.shard_map(
        functools.partial(shards, mesh.shape["ctx"], mesh.shape["head"]),
        mesh=mesh,
        in_specs=(
            P(("ctx", "head"), None),
            P(("ctx", "head"), None),
            P(("ctx", "head"), None),
            P(("ctx", "head"), None),
            P("head", "ctx"),
            P("head"),
        ),
        out_specs=(P(("ctx", "head"), None), P(("ctx", "head"), None), P(("ctx", "head"), None)),
        check_vma=False,
    )
```
